768 devices in a mesh: tile: 32 (over z_lo, x, core), bulk: 24 (over y, z_hi).
Axes of the slice: x: 4, y: 8, z: 12 (z_hi: 3, z_lo: 4; z = z_hi * 4 + z_lo), core: 2. Of those that a mesh axis runs over, the one named last changes fastest.
Arguments:
- integrals: bfloat16 [2304, 256, 768], P(('tile', 'bulk')), may hold values from -0.21875 to 0.21875
- amplitudes: bfloat16 [4, 768, 1024], P(None, 'bulk', 'tile'), may hold values from -6 to 6
- residual_in: bfloat16 [2304, 256, 1024], P(('tile', 'bulk')), may hold values from -6 to 6
- tile_irrep: int32 [2304], replicated, may hold values from 0 to 3, as said below
Outputs:
- residual: bfloat16 [2304, 256, 1024], P(('tile', 'bulk'))
The draws below stay inside these ranges and needn't reach their ends.
Inputs may be any that keep to these rules, and one draw needn't show every extreme that they name: tile_irrep never falls along the tiles, and every irrep labels at least 72 tiles.
All inputs are finite; a program needn't handle non-finite values.
Results may differ from the reference program's by a relative error of at most 0.001.
Values may be sent and summed in bfloat16 or wider, within the bound.
No kernel may reach another device: no remote copies, remote signals or barrier semaphores. Data moves between devices by JAX's collectives and lax.ppermute only.
A program may use at most 64 MiB of HBM per device.

```python
import jax
import jax.numpy as jnp
from jax import lax

V = 768
PP = 1024
IRREPS = 4
TILE = 256
ROW_TILES = 72
NT = 2304


def draw_tile_irrep(key, part):
    spare_tiles = NT - 4 * ROW_TILES
    cut_points = jnp.sort(jax.random.randint(key, (3,), 0, spare_tiles + 1))
    bounds = cut_points.astype(jnp.int32) + ROW_TILES * jnp.arange(1, 4, dtype=jnp.int32)
    positions = jnp.arange(NT, dtype=jnp.int32)
    return jnp.sum((positions[:, None] >= bounds[None, :]).astype(jnp.int32), axis=1).astype(jnp.int32)


def block_levels(key, dims, shards, smallest, largest):
    factor_of = 1.0
    for position, blocks in shards:
        steps = jax.random.uniform(jax.random.fold_in(jax.random.fold_in(key, 6), position), (blocks,), jnp.float32, smallest / len(shards), largest / len(shards))
        factor_of = factor_of * jnp.repeat(jnp.exp(steps), dims[position] // blocks).reshape((-1,) + (1,) * (len(dims) - 1 - position))
    return factor_of


def normal_values(rng, extent, scale, limit, cuts=(), held_as=jnp.bfloat16):
    array = scale * jax.random.normal(rng, extent, jnp.float32)
    if cuts:
        array = array * block_levels(rng, extent, cuts, -0.22, 0.18)
    return jnp.clip(array, -limit, limit).astype(held_as)


def setup_inputs(seed: int = 0) -> dict:
    arg_keys = jax.random.split(jax.random.key(seed), 5)
    return {
        "integrals": normal_values(arg_keys[0], (NT, TILE, V), V ** -0.5, 0.21875, ((0, 768),)),
        "amplitudes": normal_values(arg_keys[1], (IRREPS, V, PP), 1.0, 6.0, ((1, 24), (2, 32))),
        "residual_in": normal_values(arg_keys[2], (NT, TILE, PP), 1.0, 6.0, ((0, 768),)),
        "tile_irrep": draw_tile_irrep(jax.random.fold_in(arg_keys[4], 71), 0),
    }


def reference(integrals, amplitudes, residual_in, tile_irrep):
    def one_tile(operands):
        block, previous, irrep = operands
        chosen = lax.dynamic_index_in_dim(amplitudes, irrep, 0, keepdims=False)
        ladder = jnp.dot(block, chosen, preferred_element_type=jnp.float32)
        return (previous.astype(jnp.float32) + ladder).astype(jnp.bfloat16)

    return lax.map(one_tile, (integrals, residual_in, tile_irrep))
```

```python
import functools

import jax
import jax.numpy as jnp
from jax import lax
from jax.experimental import pallas as pl
from jax.experimental.pallas import tpu as pltpu
from jax.sharding import Mesh
from jax.sharding import PartitionSpec as P

CHIP_CORE = ("chip", "core")
TILE_BULK = ("chip", "core", "bulk_0", "bulk_1")
BULK = ("bulk_0", "bulk_1")


def shift(value, axis, step):
    size = lax.axis_size(axis)
    return lax.ppermute(value, axis, [(i, (i + step) % size) for i in range(size)])


def half_kernel(where_ref, integrals_ref, block_ref, previous_ref, out_ref):
    product = jnp.dot(integrals_ref[0], block_ref[0], preferred_element_type=jnp.float32)
    out_ref[0] = (previous_ref[0].astype(jnp.float32) + product).astype(out_ref.dtype)


def second_kernel(where_ref, integrals_ref, block_ref, previous_ref, so_far_ref, out_ref):
    half_kernel(where_ref, integrals_ref, block_ref, previous_ref, out_ref)


def add_half(where, integrals, block, residual_in, so_far=None):
    tiles, rows, depth = integrals.shape
    half = block.shape[2]
    strip = pl.BlockSpec((1, rows, half), lambda t, w: (t, 0, w[tiles]))
    in_specs = [
        pl.BlockSpec((1, rows, depth), lambda t, w: (t, 0, 0)),
        pl.BlockSpec((1, depth, half), lambda t, w: (w[t], 0, 0)),
        strip,
    ]
    operands = [where, integrals, block, residual_in]
    aliases = {}
    if so_far is not None:
        in_specs.append(pl.BlockSpec(memory_space=pl.ANY))
        operands.append(so_far)
        aliases = {4: 0}
    return pl.pallas_call(
        half_kernel if so_far is None else second_kernel,
        grid_spec=pltpu.PrefetchScalarGridSpec(
            num_scalar_prefetch=1, grid=(tiles,), in_specs=in_specs, out_specs=strip
        ),
        out_shape=jax.ShapeDtypeStruct(residual_in.shape, residual_in.dtype),
        input_output_aliases=aliases,
        cost_estimate=pl.CostEstimate(
            flops=2 * tiles * rows * depth * half, bytes_accessed=4_000_000, transcendentals=0
        ),
        compiler_params=pltpu.CompilerParams(vmem_limit_bytes=24 * 2**20),
    )(*operands)


def select(amplitudes, labels):
    flat = amplitudes.reshape(amplitudes.shape[0], -1)
    labels = labels[..., None]
    chosen = flat[0]
    for irrep in range(1, flat.shape[0]):
        chosen = jnp.where(labels == irrep, flat[irrep], chosen)
    return chosen


def with_slots(slots, integrals, amplitudes, residual_in, first, last, where):
    depth, width = amplitudes.shape[1:]
    chips, cores = lax.axis_size("chip"), lax.axis_size("core")
    core = lax.axis_index("core")
    wanted = jnp.minimum(first[:, None] + jnp.arange(slots, dtype=jnp.int32), last[:, None])
    wanted = jnp.repeat(wanted, cores, axis=0)
    outgoing = select(amplitudes, wanted)
    incoming = lax.all_to_all(outgoing, CHIP_CORE, split_axis=0, concat_axis=0, tiled=True)
    half = chips * cores // 2
    mine = lax.dynamic_slice_in_dim(incoming, core * half, half, 0)
    mine = mine.reshape(half, slots, depth, width).transpose(1, 2, 0, 3).reshape(slots, depth, half * width)
    z_size, z = lax.axis_size("bulk_1"), lax.axis_index("bulk_1")
    group = jnp.zeros((slots, z_size, depth, half * width), mine.dtype)
    group = lax.dynamic_update_slice_in_dim(group, mine[:, None], z, 1)
    for step in range(1, z_size):
        got = shift(mine, "bulk_1", step)
        group = lax.dynamic_update_slice_in_dim(group, got[:, None], lax.rem(z - step + z_size, z_size), 1)
    group = group.reshape(slots, z_size * depth, half * width)
    y_size, y = lax.axis_size("bulk_0"), lax.axis_index("bulk_0")
    whole = jnp.zeros((slots, y_size, z_size * depth, half * width), mine.dtype)
    whole = lax.dynamic_update_slice_in_dim(whole, group[:, None], y, 1)
    up, down = group, group
    for step in range(1, y_size // 2 + 1):
        up = shift(up, "bulk_0", 1)
        whole = lax.dynamic_update_slice_in_dim(whole, up[:, None], lax.rem(y - step + y_size, y_size), 1)
        if 2 * step < y_size:
            down = shift(down, "bulk_0", -1)
            whole = lax.dynamic_update_slice_in_dim(whole, down[:, None], lax.rem(y + step, y_size), 1)
    whole = whole.reshape(slots, y_size * z_size * depth, half * width)
    other = shift(whole, "core", 1)
    out = add_half(jnp.append(where, core), integrals, whole, residual_in)
    return add_half(jnp.append(where, 1 - core), integrals, other, residual_in, out)


def local(integrals, amplitudes, residual_in, tile_irrep):
    tile_dev = integrals.shape[0]
    chips, cores = lax.axis_size("chip"), lax.axis_size("core")
    bulk_count = lax.axis_size(BULK)
    chip, core = lax.axis_index("chip"), lax.axis_index("core")
    per_chip = tile_irrep.reshape(chips, -1)
    first, last = per_chip[:, 0], per_chip[:, -1]
    first_tile = ((chip * cores + core) * bulk_count + lax.axis_index(BULK)) * tile_dev
    labels = lax.dynamic_slice_in_dim(tile_irrep, first_tile, tile_dev, 0)
    where = labels - lax.dynamic_slice_in_dim(first, chip, 1, 0)
    operands = (integrals, amplitudes, residual_in, first, last, where)
    return lax.cond(
        jnp.max(last - first) > 1,
        functools.partial(with_slots, 3),
        functools.partial(with_slots, 2),
        *operands,
    )


def solution(mesh):
    tile, bulk = mesh.shape["tile"], mesh.shape["bulk"]
    finer = Mesh(mesh.devices.reshape(tile // 2, 2, bulk // 3, 3), TILE_BULK)
    placed = (P(TILE_BULK, None, None), P(None, BULK, CHIP_CORE), P(TILE_BULK, None, None), P())
    return jax.shard_map(
        local, mesh=finer, in_specs=placed, out_specs=P(TILE_BULK, None, None), check_vma=False
    )
```

```python
import functools

import jax
import jax.numpy as jnp
from jax import lax
from jax.experimental import pallas as pl
from jax.experimental.pallas import tpu as pltpu
from jax.sharding import Mesh
from jax.sharding import PartitionSpec as P

CHIP_CORE = ("chip", "core")
TILE_BULK = ("chip", "core", "bulk_0", "bulk_1")
BULK = ("bulk_0", "bulk_1")
VMEM = pl.BlockSpec(memory_space=pltpu.VMEM)
SMEM = pl.BlockSpec(memory_space=pltpu.SMEM)


def shift(value, axis, step):
    size = lax.axis_size(axis)
    return lax.ppermute(value, axis, [(i, (i + step) % size) for i in range(size)])


def choose_kernel(slots, chips, tiles, bulk_0, bulk_1, labels_ref, packed_ref, outgoing_ref, where_ref):
    per_chip = labels_ref.shape[0] // chips
    rows = packed_ref.shape[1]
    most = jnp.int32(0)
    for chip in range(chips):
        first, last = labels_ref[chip * per_chip], labels_ref[(chip + 1) * per_chip - 1]
        most = jnp.maximum(most, last - first)
        for slot in range(slots):
            block = packed_ref[jnp.minimum(first + slot, last)]
            for core in range(2):
                outgoing_ref[2 * chip + core, pl.ds(slot * rows, rows), :] = block
    own = lax.axis_index("chip")
    row = own * 2 + lax.axis_index("core")
    column = lax.axis_index("bulk_0") * bulk_1 + lax.axis_index("bulk_1")
    first_tile = (row * (bulk_0 * bulk_1) + column) * tiles
    for t in range(tiles):
        where_ref[t] = labels_ref[first_tile + t] - labels_ref[own * per_chip]
    where_ref[tiles] = most + 1


def choose(slots, labels, packed, tiles):
    chips = lax.axis_size("chip")
    rows, lanes = packed.shape[1:]
    body = functools.partial(
        choose_kernel, slots, chips, tiles, lax.axis_size("bulk_0"), lax.axis_size("bulk_1")
    )
    return pl.pallas_call(
        body,
        in_specs=[SMEM, VMEM],
        out_specs=(VMEM, SMEM),
        out_shape=(
            jax.ShapeDtypeStruct((2 * chips, slots * rows, lanes), packed.dtype),
            jax.ShapeDtypeStruct((tiles + 1,), jnp.int32),
        ),
    )(labels, packed)


def ladder_kernel(where_ref, integrals_ref, own_ref, other_ref, previous_ref, out_ref, strip_ref, sems):
    tiles = integrals_ref.shape[0]
    half = own_ref.shape[2]
    core = lax.axis_index("core")
    chunk = 256
    copies = []
    for t in range(tiles):
        slot = where_ref[t]
        for block_ref, side in ((own_ref, core), (other_ref, 1 - core)):
            for begin in range(0, half, chunk):
                columns = pl.ds(pl.multiple_of(side * half + begin, chunk), chunk)
                product = jnp.dot(
                    integrals_ref[t], block_ref[slot, :, begin : begin + chunk], preferred_element_type=jnp.float32
                )
                total = previous_ref[t, :, columns].astype(jnp.float32) + product
                strip_ref[t, :, columns] = total.astype(strip_ref.dtype)
        copies.append(pltpu.make_async_copy(strip_ref.at[t], out_ref.at[t], sems.at[t]))
        copies[-1].start()
    for copy in copies:
        copy.wait()


def ladder(where, integrals, own, other, residual_in):
    tiles, rows, depth = integrals.shape
    return pl.pallas_call(
        ladder_kernel,
        in_specs=[SMEM, VMEM, VMEM, VMEM, VMEM],
        out_specs=pl.BlockSpec(memory_space=pl.ANY),
        out_shape=jax.ShapeDtypeStruct(residual_in.shape, residual_in.dtype),
        scratch_shapes=[
            pltpu.VMEM(residual_in.shape, residual_in.dtype),
            pltpu.SemaphoreType.DMA((tiles,)),
        ],
        compiler_params=pltpu.CompilerParams(vmem_limit_bytes=24 * 2**20),
    )(where, integrals, own, other, residual_in)


def with_slots(slots, outgoing, where, integrals, residual_in, depth, width):
    chips = lax.axis_size("chip")
    core = lax.axis_index("core")
    incoming = lax.all_to_all(outgoing, CHIP_CORE, split_axis=0, concat_axis=0, tiled=True)
    half = chips
    mine = lax.dynamic_slice_in_dim(incoming, core * half, half, 0)
    parts = incoming.shape[2] // width
    mine = mine.reshape(half, slots, depth // parts, parts, width).transpose(1, 2, 3, 0, 4)
    mine = mine.reshape(slots, depth, half * width)
    z_size, z = lax.axis_size("bulk_1"), lax.axis_index("bulk_1")
    group = jnp.zeros((slots, z_size, depth, half * width), mine.dtype)
    group = lax.dynamic_update_slice_in_dim(group, mine[:, None], z, 1)
    for step in range(1, z_size):
        got = shift(mine, "bulk_1", step)
        group = lax.dynamic_update_slice_in_dim(group, got[:, None], lax.rem(z - step + z_size, z_size), 1)
    group = group.reshape(slots, z_size * depth, half * width)
    y_size, y = lax.axis_size("bulk_0"), lax.axis_index("bulk_0")
    whole = jnp.zeros((slots, y_size, z_size * depth, half * width), mine.dtype)
    whole = lax.dynamic_update_slice_in_dim(whole, group[:, None], y, 1)
    up, down = group, group
    for step in range(1, y_size // 2):
        up = shift(up, "bulk_0", 1)
        whole = lax.dynamic_update_slice_in_dim(whole, up[:, None], lax.rem(y - step + y_size, y_size), 1)
        down = shift(down, "bulk_0", -1)
        whole = lax.dynamic_update_slice_in_dim(whole, down[:, None], lax.rem(y + step, y_size), 1)
    up = shift(up, "bulk_0", 1)
    far = lax.rem(y + y_size // 2, y_size)
    other = shift(whole, "core", 1)
    whole = lax.dynamic_update_slice_in_dim(whole, up[:, None], far, 1)
    other = lax.dynamic_update_slice_in_dim(other, shift(up, "core", 1)[:, None], far, 1)
    flat = (slots, y_size * z_size * depth, half * width)
    return ladder(where, integrals, whole.reshape(flat), other.reshape(flat), residual_in)


def local(integrals, amplitudes, residual_in, tile_irrep):
    tiles = integrals.shape[0]
    irreps, depth, width = amplitudes.shape
    parts = 128 // width
    packed = amplitudes.reshape(irreps, depth // parts, parts * width)
    outgoing, where = choose(2, tile_irrep, packed, tiles)

    def two():
        return with_slots(2, outgoing, where, integrals, residual_in, depth, width)

    def three():
        return with_slots(3, *choose(3, tile_irrep, packed, tiles), integrals, residual_in, depth, width)

    return lax.cond(where[tiles] > 2, three, two)


def solution(mesh):
    tile, bulk = mesh.shape["tile"], mesh.shape["bulk"]
    finer = Mesh(mesh.devices.reshape(tile // 2, 2, bulk // 3, 3), TILE_BULK)
    placed = (P(TILE_BULK, None, None), P(None, BULK, CHIP_CORE), P(TILE_BULK, None, None), P())
    return jax.shard_map(
        local, mesh=finer, in_specs=placed, out_specs=P(TILE_BULK, None, None), check_vma=False
    )
```

```python
import functools

import jax
import jax.numpy as jnp
from jax import lax
from jax.experimental import pallas as pl
from jax.experimental.pallas import tpu as pltpu
from jax.sharding import Mesh
from jax.sharding import PartitionSpec as P

CHIP_CORE = ("chip", "core")
TILE_BULK = ("chip", "core", "bulk_0", "bulk_1")
BULK = ("bulk_0", "bulk_1")
VMEM = pl.BlockSpec(memory_space=pltpu.VMEM)
SMEM = pl.BlockSpec(memory_space=pltpu.SMEM)


def shift(value, axis, step):
    size = lax.axis_size(axis)
    return lax.ppermute(value, axis, [(i, (i + step) % size) for i in range(size)])


def choose_kernel(slots, chips, tiles, bulk_0, bulk_1, labels_ref, amplitudes_ref, outgoing_ref, where_ref, packed_ref):
    per_chip = labels_ref.shape[0] // chips
    irreps, rows, lanes = packed_ref.shape
    for irrep in range(irreps):
        block = amplitudes_ref[irrep].astype(jnp.float32)
        pieces = [block[begin : begin + rows] for begin in range(0, block.shape[0], rows)]
        packed_ref[irrep] = jnp.concatenate(pieces, axis=1)
    most = jnp.int32(0)
    for chip in range(chips):
        first, last = labels_ref[chip * per_chip], labels_ref[(chip + 1) * per_chip - 1]
        most = jnp.maximum(most, last - first)
        chosen = [packed_ref[jnp.minimum(first + slot, last)] for slot in range(slots)]
        chosen = jnp.concatenate(chosen, axis=0).astype(outgoing_ref.dtype)
        for core in range(2):
            outgoing_ref[2 * chip + core] = chosen
    own = lax.axis_index("chip")
    row = own * 2 + lax.axis_index("core")
    column = lax.axis_index("bulk_0") * bulk_1 + lax.axis_index("bulk_1")
    first_tile = (row * (bulk_0 * bulk_1) + column) * tiles
    for t in range(tiles):
        where_ref[t] = labels_ref[first_tile + t] - labels_ref[own * per_chip]
    where_ref[tiles] = most + 1


def choose(slots, labels, amplitudes, tiles):
    chips = lax.axis_size("chip")
    irreps, depth, width = amplitudes.shape
    lanes = 128
    rows = depth * width // lanes
    body = functools.partial(
        choose_kernel, slots, chips, tiles, lax.axis_size("bulk_0"), lax.axis_size("bulk_1")
    )
    return pl.pallas_call(
        body,
        in_specs=[SMEM, VMEM],
        out_specs=(VMEM, SMEM),
        out_shape=(
            jax.ShapeDtypeStruct((2 * chips, slots * rows, lanes), amplitudes.dtype),
            jax.ShapeDtypeStruct((tiles + 1,), jnp.int32),
        ),
        scratch_shapes=[pltpu.VMEM((irreps, rows, lanes), jnp.float32)],
    )(labels, amplitudes)


def begin_kernel(other, where_ref, integrals_ref, block_ref, previous_ref, out_ref):
    tiles = integrals_ref.shape[0]
    half = block_ref.shape[2]
    core = lax.axis_index("core")
    side = 1 - core if other else core
    chunk = 256
    for t in range(tiles):
        slot = where_ref[t]
        for begin in range(0, half, chunk):
            columns = pl.ds(pl.multiple_of(side * half + begin, chunk), chunk)
            product = jnp.dot(
                integrals_ref[t], block_ref[slot, :, begin : begin + chunk], preferred_element_type=jnp.float32
            )
            out_ref[t, :, begin : begin + chunk] = previous_ref[t, :, columns].astype(jnp.float32) + product


def begin_half(other, where, integrals, block, residual_in):
    tiles, rows, depth = integrals.shape
    half = block.shape[2]
    return pl.pallas_call(
        functools.partial(begin_kernel, other),
        in_specs=[SMEM, VMEM, VMEM, VMEM],
        out_specs=VMEM,
        out_shape=jax.ShapeDtypeStruct((tiles, rows, half), jnp.float32),
        cost_estimate=pl.CostEstimate(
            flops=2 * tiles * rows * depth * half, bytes_accessed=4_000_000, transcendentals=0
        ),
        compiler_params=pltpu.CompilerParams(vmem_limit_bytes=24 * 2**20),
    )(where, integrals, block, residual_in)


def finish_kernel(where_ref, strip_ref, own_ref, other_ref, own_sum_ref, other_sum_ref, out_ref, rows_ref, sems):
    tiles, _, half = own_sum_ref.shape
    core = lax.axis_index("core")
    copies = []
    for t in range(tiles):
        slot = where_ref[t]
        for block_ref, sum_ref, side in ((own_ref, own_sum_ref, core), (other_ref, other_sum_ref, 1 - core)):
            columns = pl.ds(pl.multiple_of(side * half, half), half)
            product = jnp.dot(strip_ref[t], block_ref[slot], preferred_element_type=jnp.float32)
            rows_ref[t, :, columns] = (sum_ref[t] + product).astype(rows_ref.dtype)
        copies.append(pltpu.make_async_copy(rows_ref.at[t], out_ref.at[t], sems.at[t]))
        copies[-1].start()
    for copy in copies:
        copy.wait()


def finish(where, strip, own, other, own_sum, other_sum, like):
    tiles = like.shape[0]
    return pl.pallas_call(
        finish_kernel,
        in_specs=[SMEM] + [VMEM] * 5,
        out_specs=pl.BlockSpec(memory_space=pl.ANY),
        out_shape=jax.ShapeDtypeStruct(like.shape, like.dtype),
        scratch_shapes=[pltpu.VMEM(like.shape, like.dtype), pltpu.SemaphoreType.DMA((tiles,))],
        compiler_params=pltpu.CompilerParams(vmem_limit_bytes=24 * 2**20),
    )(where, strip, own, other, own_sum, other_sum)


def with_slots(slots, incoming, where, integrals, residual_in, depth, width):
    half = lax.axis_size("chip")
    core = lax.axis_index("core")
    mine = lax.dynamic_slice_in_dim(incoming, core * half, half, 0)
    parts = incoming.shape[2] // width
    mine = mine.reshape(half, slots, depth // parts, parts, width).transpose(1, 3, 2, 0, 4)
    mine = mine.reshape(slots, depth, half * width)
    z_size, z = lax.axis_size("bulk_1"), lax.axis_index("bulk_1")
    group = jnp.zeros((slots, z_size, depth, half * width), mine.dtype)
    group = lax.dynamic_update_slice_in_dim(group, mine[:, None], z, 1)
    for step in range(1, z_size):
        got = shift(mine, "bulk_1", step)
        group = lax.dynamic_update_slice_in_dim(group, got[:, None], lax.rem(z - step + z_size, z_size), 1)
    group = group.reshape(slots, z_size * depth, half * width)
    y_size, y = lax.axis_size("bulk_0"), lax.axis_index("bulk_0")
    whole = jnp.zeros((slots, y_size, z_size * depth, half * width), mine.dtype)
    whole = lax.dynamic_update_slice_in_dim(whole, group[:, None], y, 1)
    up, down = group, group
    for step in range(1, y_size // 2):
        up = shift(up, "bulk_0", 1)
        whole = lax.dynamic_update_slice_in_dim(whole, up[:, None], lax.rem(y - step + y_size, y_size), 1)
        down = shift(down, "bulk_0", -1)
        whole = lax.dynamic_update_slice_in_dim(whole, down[:, None], lax.rem(y + step, y_size), 1)
    whole = whole.reshape(slots, y_size * z_size * depth, half * width)
    up = shift(up, "bulk_0", 1)
    own_sum = begin_half(False, where, integrals, whole, residual_in)
    up, own_sum = lax.optimization_barrier((up, own_sum))
    other_sum = begin_half(True, where, integrals, shift(whole, "core", 1), residual_in)
    far = lax.rem(y + y_size // 2, y_size)
    strip = lax.dynamic_slice_in_dim(integrals, far * (z_size * depth), z_size * depth, 2)
    return finish(where, strip, up, shift(up, "core", 1), own_sum, other_sum, residual_in)


def local(integrals, amplitudes, residual_in, tile_irrep):
    tiles = integrals.shape[0]
    _, depth, width = amplitudes.shape

    def spread(outgoing):
        return lax.all_to_all(outgoing, CHIP_CORE, split_axis=0, concat_axis=0, tiled=True)

    outgoing, where = choose(2, tile_irrep, amplitudes, tiles)
    incoming = spread(outgoing)

    def two():
        return with_slots(2, incoming, where, integrals, residual_in, depth, width)

    def three():
        wider = spread(choose(3, tile_irrep, amplitudes, tiles)[0])
        return with_slots(3, wider, where, integrals, residual_in, depth, width)

    return lax.cond(where[tiles] > 2, three, two)


def solution(mesh):
    tile, bulk = mesh.shape["tile"], mesh.shape["bulk"]
    finer = Mesh(mesh.devices.reshape(tile // 2, 2, bulk // 3, 3), TILE_BULK)
    placed = (P(TILE_BULK, None, None), P(None, BULK, CHIP_CORE), P(TILE_BULK, None, None), P())
    return jax.shard_map(
        local, mesh=finer, in_specs=placed, out_specs=P(TILE_BULK, None, None), check_vma=False
    )
```

```python
import functools

import jax
import jax.numpy as jnp
from jax import lax
from jax.experimental import pallas as pl
from jax.experimental.pallas import tpu as pltpu
from jax.sharding import Mesh
from jax.sharding import PartitionSpec as P

CHIP_CORE = ("chip", "core")
TILE_BULK = ("chip", "core", "bulk_0", "bulk_1")
BULK = ("bulk_0", "bulk_1")
VMEM = pl.BlockSpec(memory_space=pltpu.VMEM)
SMEM = pl.BlockSpec(memory_space=pltpu.SMEM)
ANY = pl.BlockSpec(memory_space=pl.ANY)


def shift(value, axis, step):
    size = lax.axis_size(axis)
    return lax.ppermute(value, axis, [(i, (i + step) % size) for i in range(size)])


def choose_kernel(slots, chips, tiles, bulk_0, bulk_1, labels_ref, amplitudes_ref, outgoing_ref, where_ref, packed_ref):
    per_chip = labels_ref.shape[0] // chips
    irreps, rows, lanes = packed_ref.shape
    for irrep in range(irreps):
        block = amplitudes_ref[irrep].astype(jnp.float32)
        pieces = [block[begin : begin + rows] for begin in range(0, block.shape[0], rows)]
        packed_ref[irrep] = jnp.concatenate(pieces, axis=1)
    most = jnp.int32(0)
    for chip in range(chips):
        first, last = labels_ref[chip * per_chip], labels_ref[(chip + 1) * per_chip - 1]
        most = jnp.maximum(most, last - first)
        chosen = [packed_ref[jnp.minimum(first + slot, last)] for slot in range(slots)]
        chosen = jnp.concatenate(chosen, axis=0).astype(outgoing_ref.dtype)
        for core in range(2):
            outgoing_ref[2 * chip + core] = chosen
    own = lax.axis_index("chip")
    row = own * 2 + lax.axis_index("core")
    column = lax.axis_index("bulk_0") * bulk_1 + lax.axis_index("bulk_1")
    first_tile = (row * (bulk_0 * bulk_1) + column) * tiles
    for t in range(tiles):
        where_ref[t] = labels_ref[first_tile + t] - labels_ref[own * per_chip]
    where_ref[tiles] = most + 1


def choose(slots, labels, amplitudes, tiles):
    chips = lax.axis_size("chip")
    irreps, depth, width = amplitudes.shape
    lanes = 128
    rows = depth * width // lanes
    body = functools.partial(
        choose_kernel, slots, chips, tiles, lax.axis_size("bulk_0"), lax.axis_size("bulk_1")
    )
    return pl.pallas_call(
        body,
        in_specs=[SMEM, VMEM],
        out_specs=(VMEM, SMEM),
        out_shape=(
            jax.ShapeDtypeStruct((2 * chips, slots * rows, lanes), amplitudes.dtype),
            jax.ShapeDtypeStruct((tiles + 1,), jnp.int32),
        ),
        scratch_shapes=[pltpu.VMEM((irreps, rows, lanes), jnp.float32)],
    )(labels, amplitudes)


def half_kernel(where_ref, integrals_ref, block_ref, previous_ref, side, begin, strip_ref, out_ref, sems):
    tiles, _, half = strip_ref.shape
    chunk = 256
    copies = []
    for t in range(tiles):
        slot = where_ref[t]
        for offset in range(0, half, chunk):
            columns = pl.ds(pl.multiple_of(begin + offset, chunk), chunk)
            product = jnp.dot(
                integrals_ref[t], block_ref[slot, :, offset : offset + chunk], preferred_element_type=jnp.float32
            )
            total = previous_ref[t, :, columns].astype(jnp.float32) + product
            strip_ref[t, :, offset : offset + chunk] = total.astype(strip_ref.dtype)
        target = out_ref.at[t, :, pl.ds(pl.multiple_of(side * half, half), half)]
        copies.append(pltpu.make_async_copy(strip_ref.at[t], target, sems.at[t]))
        copies[-1].start()
    return copies


def own_kernel(
    where_ref, integrals_ref, block_ref, previous_ref, out_ref, kept_integrals_ref, kept_previous_ref, strip_ref, sems
):
    half = block_ref.shape[2]
    side = lax.axis_index("core")
    copies = half_kernel(where_ref, integrals_ref, block_ref, previous_ref, side, side * half, strip_ref, out_ref, sems)
    kept_integrals_ref[...] = integrals_ref[...]
    kept_previous_ref[...] = previous_ref[:, :, pl.ds(pl.multiple_of((1 - side) * half, half), half)]
    for copy in copies:
        copy.wait()


def other_kernel(where_ref, integrals_ref, block_ref, previous_ref, so_far_ref, out_ref, strip_ref, sems):
    side = 1 - lax.axis_index("core")
    for copy in half_kernel(where_ref, integrals_ref, block_ref, previous_ref, side, 0, strip_ref, out_ref, sems):
        copy.wait()


def scratch(tiles, rows, half, dtype):
    return [pltpu.VMEM((tiles, rows, half), dtype), pltpu.SemaphoreType.DMA((tiles,))]


def own_half(where, integrals, block, residual_in):
    tiles, rows, depth = integrals.shape
    half = block.shape[2]
    return pl.pallas_call(
        own_kernel,
        in_specs=[SMEM, VMEM, VMEM, VMEM],
        out_specs=(ANY, VMEM, VMEM),
        out_shape=(
            jax.ShapeDtypeStruct(residual_in.shape, residual_in.dtype),
            jax.ShapeDtypeStruct(integrals.shape, integrals.dtype),
            jax.ShapeDtypeStruct((tiles, rows, half), residual_in.dtype),
        ),
        scratch_shapes=scratch(tiles, rows, half, residual_in.dtype),
        cost_estimate=pl.CostEstimate(
            flops=2 * tiles * rows * depth * half, bytes_accessed=4_000_000, transcendentals=0
        ),
        compiler_params=pltpu.CompilerParams(vmem_limit_bytes=24 * 2**20),
    )(where, integrals, block, residual_in)


def other_half(where, integrals, block, previous, so_far):
    return pl.pallas_call(
        other_kernel,
        in_specs=[SMEM, VMEM, VMEM, VMEM, ANY],
        out_specs=ANY,
        out_shape=jax.ShapeDtypeStruct(so_far.shape, so_far.dtype),
        scratch_shapes=scratch(*previous.shape, so_far.dtype),
        input_output_aliases={4: 0},
        compiler_params=pltpu.CompilerParams(vmem_limit_bytes=24 * 2**20),
    )(where, integrals, block, previous, so_far)


def put(whole, block, at):
    return lax.dynamic_update_slice_in_dim(whole, block[:, None], lax.rem(at + whole.shape[1], whole.shape[1]), 1)


def with_slots(slots, incoming, where, integrals, residual_in, depth, width):
    half = lax.axis_size("chip")
    core = lax.axis_index("core")
    mine = lax.dynamic_slice_in_dim(incoming, core * half, half, 0)
    parts = incoming.shape[2] // width
    mine = mine.reshape(half, slots, depth // parts, parts, width).transpose(1, 3, 2, 0, 4)
    mine = mine.reshape(slots, depth, half * width)
    z_size, z = lax.axis_size("bulk_1"), lax.axis_index("bulk_1")
    group = jnp.zeros((slots, z_size, depth, half * width), mine.dtype)
    group = lax.dynamic_update_slice_in_dim(group, mine[:, None], z, 1)
    for step in range(1, z_size):
        got = shift(mine, "bulk_1", step)
        group = lax.dynamic_update_slice_in_dim(group, got[:, None], lax.rem(z - step + z_size, z_size), 1)
    group = group.reshape(slots, z_size * depth, half * width)
    y_size, y = lax.axis_size("bulk_0"), lax.axis_index("bulk_0")
    whole = jnp.zeros((slots, y_size, z_size * depth, half * width), mine.dtype)
    whole = put(whole, group, y)
    up, down = group, group
    for step in range(1, y_size // 2 - 1):
        up, down = shift(up, "bulk_0", 1), shift(down, "bulk_0", -1)
        whole = put(put(whole, up, y - step), down, y + step)
    last = y_size // 2 - 1
    up, far, down = shift(up, "bulk_0", 1), shift(up, "bulk_0", 2), shift(down, "bulk_0", -1)
    whole = put(put(put(whole, up, y - last), down, y + last), far, y + last + 1)
    other = shift(whole, "core", 1)
    flat = (slots, y_size * z_size * depth, half * width)
    out, integrals, previous = own_half(where, integrals, whole.reshape(flat), residual_in)
    return other_half(where, integrals, other.reshape(flat), previous, out)


def local(integrals, amplitudes, residual_in, tile_irrep):
    tiles = integrals.shape[0]
    _, depth, width = amplitudes.shape

    def spread(outgoing):
        return lax.all_to_all(outgoing, CHIP_CORE, split_axis=0, concat_axis=0, tiled=True)

    outgoing, where = choose(2, tile_irrep, amplitudes, tiles)
    incoming = spread(outgoing)

    def two():
        return with_slots(2, incoming, where, integrals, residual_in, depth, width)

    def three():
        wider = spread(choose(3, tile_irrep, amplitudes, tiles)[0])
        return with_slots(3, wider, where, integrals, residual_in, depth, width)

    return lax.cond(where[tiles] > 2, three, two)


def solution(mesh):
    tile, bulk = mesh.shape["tile"], mesh.shape["bulk"]
    finer = Mesh(mesh.devices.reshape(tile // 2, 2, bulk // 3, 3), TILE_BULK)
    placed = (P(TILE_BULK, None, None), P(None, BULK, CHIP_CORE), P(TILE_BULK, None, None), P())
    return jax.shard_map(
        local, mesh=finer, in_specs=placed, out_specs=P(TILE_BULK, None, None), check_vma=False
    )
```

```python
import functools

import jax
import jax.numpy as jnp
from jax import lax
from jax.experimental import pallas as pl
from jax.experimental.pallas import tpu as pltpu
from jax.sharding import Mesh
from jax.sharding import PartitionSpec as P

CHIP_CORE = ("chip", "core")
TILE_BULK = ("chip", "core", "bulk_0", "bulk_1")
BULK = ("bulk_0", "bulk_1")
VMEM = pl.BlockSpec(memory_space=pltpu.VMEM)
SMEM = pl.BlockSpec(memory_space=pltpu.SMEM)
ANY = pl.BlockSpec(memory_space=pl.ANY)


def shift(value, axis, step):
    size = lax.axis_size(axis)
    return lax.ppermute(value, axis, [(i, (i + step) % size) for i in range(size)])


def choose_kernel(slots, chips, tiles, bulk_0, bulk_1, labels_ref, amplitudes_ref, outgoing_ref, where_ref, packed_ref):
    per_chip = labels_ref.shape[0] // chips
    irreps, rows, lanes = packed_ref.shape
    for irrep in range(irreps):
        block = amplitudes_ref[irrep].astype(jnp.float32)
        pieces = [block[begin : begin + rows] for begin in range(0, block.shape[0], rows)]
        packed_ref[irrep] = jnp.concatenate(pieces, axis=1)
    most = jnp.int32(0)
    for chip in range(chips):
        first, last = labels_ref[chip * per_chip], labels_ref[(chip + 1) * per_chip - 1]
        most = jnp.maximum(most, last - first)
        chosen = [packed_ref[jnp.minimum(first + slot, last)] for slot in range(slots)]
        chosen = jnp.concatenate(chosen, axis=0).astype(outgoing_ref.dtype)
        for core in range(2):
            outgoing_ref[2 * chip + core] = chosen
    own = lax.axis_index("chip")
    row = own * 2 + lax.axis_index("core")
    column = lax.axis_index("bulk_0") * bulk_1 + lax.axis_index("bulk_1")
    first_tile = (row * (bulk_0 * bulk_1) + column) * tiles
    for t in range(tiles):
        where_ref[t] = labels_ref[first_tile + t] - labels_ref[own * per_chip]
    where_ref[tiles] = most + 1


def choose(slots, labels, amplitudes, tiles):
    chips = lax.axis_size("chip")
    irreps, depth, width = amplitudes.shape
    lanes = 128
    rows = depth * width // lanes
    body = functools.partial(
        choose_kernel, slots, chips, tiles, lax.axis_size("bulk_0"), lax.axis_size("bulk_1")
    )
    return pl.pallas_call(
        body,
        in_specs=[SMEM, VMEM],
        out_specs=(VMEM, SMEM),
        out_shape=(
            jax.ShapeDtypeStruct((2 * chips, slots * rows, lanes), amplitudes.dtype),
            jax.ShapeDtypeStruct((tiles + 1,), jnp.int32),
        ),
        scratch_shapes=[pltpu.VMEM((irreps, rows, lanes), jnp.float32)],
    )(labels, amplitudes)


def half_kernel(where_ref, integrals_ref, block_ref, previous_ref, side, begin, strip_ref, out_ref, sems):
    tiles, _, half = strip_ref.shape
    chunk = 256
    copies = []
    for t in range(tiles):
        slot = where_ref[t]
        for offset in range(0, half, chunk):
            columns = pl.ds(pl.multiple_of(begin + offset, chunk), chunk)
            product = jnp.dot(
                integrals_ref[t], block_ref[slot, :, offset : offset + chunk], preferred_element_type=jnp.float32
            )
            total = previous_ref[t, :, columns].astype(jnp.float32) + product
            strip_ref[t, :, offset : offset + chunk] = total.astype(strip_ref.dtype)
        target = out_ref.at[t, :, pl.ds(pl.multiple_of(side * half, half), half)]
        copies.append(pltpu.make_async_copy(strip_ref.at[t], target, sems.at[t]))
        copies[-1].start()
    return copies


def own_kernel(
    where_ref, integrals_ref, block_ref, previous_ref, out_ref, kept_integrals_ref, kept_previous_ref, strip_ref, sems
):
    half = block_ref.shape[2]
    side = lax.axis_index("core")
    copies = half_kernel(where_ref, integrals_ref, block_ref, previous_ref, side, side * half, strip_ref, out_ref, sems)
    kept_integrals_ref[...] = integrals_ref[...]
    kept_previous_ref[...] = previous_ref[:, :, pl.ds(pl.multiple_of((1 - side) * half, half), half)]
    for copy in copies:
        copy.wait()


def other_kernel(where_ref, integrals_ref, block_ref, previous_ref, so_far_ref, out_ref, strip_ref, sems):
    side = 1 - lax.axis_index("core")
    for copy in half_kernel(where_ref, integrals_ref, block_ref, previous_ref, side, 0, strip_ref, out_ref, sems):
        copy.wait()


def scratch(tiles, rows, half, dtype):
    return [pltpu.VMEM((tiles, rows, half), dtype), pltpu.SemaphoreType.DMA((tiles,))]


def own_half(where, integrals, block, residual_in):
    tiles, rows, depth = integrals.shape
    half = block.shape[2]
    return pl.pallas_call(
        own_kernel,
        in_specs=[SMEM, VMEM, VMEM, VMEM],
        out_specs=(ANY, VMEM, VMEM),
        out_shape=(
            jax.ShapeDtypeStruct(residual_in.shape, residual_in.dtype),
            jax.ShapeDtypeStruct(integrals.shape, integrals.dtype),
            jax.ShapeDtypeStruct((tiles, rows, half), residual_in.dtype),
        ),
        scratch_shapes=scratch(tiles, rows, half, residual_in.dtype),
        cost_estimate=pl.CostEstimate(
            flops=2 * tiles * rows * depth * half, bytes_accessed=4_000_000, transcendentals=0
        ),
        compiler_params=pltpu.CompilerParams(vmem_limit_bytes=24 * 2**20),
    )(where, integrals, block, residual_in)


def other_half(where, integrals, block, previous, so_far):
    return pl.pallas_call(
        other_kernel,
        in_specs=[SMEM, VMEM, VMEM, VMEM, ANY],
        out_specs=ANY,
        out_shape=jax.ShapeDtypeStruct(so_far.shape, so_far.dtype),
        scratch_shapes=scratch(*previous.shape, so_far.dtype),
        input_output_aliases={4: 0},
        compiler_params=pltpu.CompilerParams(vmem_limit_bytes=24 * 2**20),
    )(where, integrals, block, previous, so_far)


def put(whole, block, at):
    return lax.dynamic_update_slice_in_dim(whole, block[:, None], lax.rem(at + whole.shape[1], whole.shape[1]), 1)


def with_slots(slots, incoming, where, integrals, residual_in, depth, width):
    half = lax.axis_size("chip")
    core = lax.axis_index("core")
    mine = lax.dynamic_slice_in_dim(incoming, core * half, half, 0)
    parts = incoming.shape[2] // width
    mine = mine.reshape(half, slots, depth // parts, parts, width).transpose(1, 3, 2, 0, 4)
    mine = mine.reshape(slots, depth, half * width)
    z_size, z = lax.axis_size("bulk_1"), lax.axis_index("bulk_1")
    group = jnp.zeros((slots, z_size, depth, half * width), mine.dtype)
    group = lax.dynamic_update_slice_in_dim(group, mine[:, None], z, 1)
    for step in range(1, z_size):
        got = shift(mine, "bulk_1", step)
        group = lax.dynamic_update_slice_in_dim(group, got[:, None], lax.rem(z - step + z_size, z_size), 1)
    group = group.reshape(slots, z_size * depth, half * width)
    y_size, y = lax.axis_size("bulk_0"), lax.axis_index("bulk_0")
    whole = jnp.zeros((slots, y_size, z_size * depth, half * width), mine.dtype)
    whole = put(whole, group, y)
    up, down = group, group
    for step in range(1, y_size // 2 - 1):
        up, down = shift(up, "bulk_0", 1), shift(down, "bulk_0", -1)
        whole = put(put(whole, up, y - step), down, y + step)
    last = y_size // 2 - 1
    far, up, down = shift(down, "bulk_0", -2), shift(up, "bulk_0", 1), shift(down, "bulk_0", -1)
    whole = put(put(put(whole, up, y - last), down, y + last), far, y + last + 1)
    other = shift(whole, "core", 1)
    flat = (slots, y_size * z_size * depth, half * width)
    out, integrals, previous = own_half(where, integrals, whole.reshape(flat), residual_in)
    return other_half(where, integrals, other.reshape(flat), previous, out)


def local(integrals, amplitudes, residual_in, tile_irrep):
    tiles = integrals.shape[0]
    _, depth, width = amplitudes.shape

    def spread(outgoing):
        return lax.all_to_all(outgoing, CHIP_CORE, split_axis=0, concat_axis=0, tiled=True)

    outgoing, where = choose(2, tile_irrep, amplitudes, tiles)
    incoming = spread(outgoing)

    def two():
        return with_slots(2, incoming, where, integrals, residual_in, depth, width)

    def three():
        wider = spread(choose(3, tile_irrep, amplitudes, tiles)[0])
        return with_slots(3, wider, where, integrals, residual_in, depth, width)

    return lax.cond(where[tiles] > 2, three, two)


def solution(mesh):
    tile, bulk = mesh.shape["tile"], mesh.shape["bulk"]
    finer = Mesh(mesh.devices.reshape(tile // 2, 2, bulk // 3, 3), TILE_BULK)
    placed = (P(TILE_BULK, None, None), P(None, BULK, CHIP_CORE), P(TILE_BULK, None, None), P())
    return jax.shard_map(
        local, mesh=finer, in_specs=placed, out_specs=P(TILE_BULK, None, None), check_vma=False
    )
```

```python
import functools

import jax
import jax.numpy as jnp
from jax import lax
from jax.experimental import pallas as pl
from jax.experimental.pallas import tpu as pltpu
from jax.sharding import Mesh
from jax.sharding import PartitionSpec as P

CHIP_CORE = ("chip", "core")
TILE_BULK = ("chip", "core", "bulk_0", "bulk_1")
BULK = ("bulk_0", "bulk_1")
VMEM = pl.BlockSpec(memory_space=pltpu.VMEM)
SMEM = pl.BlockSpec(memory_space=pltpu.SMEM)
ANY = pl.BlockSpec(memory_space=pl.ANY)


def shift(value, axis, step):
    size = lax.axis_size(axis)
    return lax.ppermute(value, axis, [(i, (i + step) % size) for i in range(size)])


def choose_kernel(slots, chips, tiles, bulk_0, bulk_1, labels_ref, amplitudes_ref, outgoing_ref, where_ref, packed_ref):
    per_chip = labels_ref.shape[0] // chips
    irreps, rows, lanes = packed_ref.shape
    for irrep in range(irreps):
        block = amplitudes_ref[irrep].astype(jnp.float32)
        pieces = [block[begin : begin + rows] for begin in range(0, block.shape[0], rows)]
        packed_ref[irrep] = jnp.concatenate(pieces, axis=1)
    most = jnp.int32(0)
    for chip in range(chips):
        first, last = labels_ref[chip * per_chip], labels_ref[(chip + 1) * per_chip - 1]
        most = jnp.maximum(most, last - first)
        chosen = [packed_ref[jnp.minimum(first + slot, last)] for slot in range(slots)]
        chosen = jnp.concatenate(chosen, axis=0).astype(outgoing_ref.dtype)
        for core in range(2):
            outgoing_ref[2 * chip + core] = chosen
    own = lax.axis_index("chip")
    row = own * 2 + lax.axis_index("core")
    column = lax.axis_index("bulk_0") * bulk_1 + lax.axis_index("bulk_1")
    first_tile = (row * (bulk_0 * bulk_1) + column) * tiles
    for t in range(tiles):
        where_ref[t] = labels_ref[first_tile + t] - labels_ref[own * per_chip]
    where_ref[tiles] = most + 1


def choose(slots, labels, amplitudes, tiles):
    chips = lax.axis_size("chip")
    irreps, depth, width = amplitudes.shape
    lanes = 128
    rows = depth * width // lanes
    body = functools.partial(
        choose_kernel, slots, chips, tiles, lax.axis_size("bulk_0"), lax.axis_size("bulk_1")
    )
    return pl.pallas_call(
        body,
        in_specs=[SMEM, VMEM],
        out_specs=(VMEM, SMEM),
        out_shape=(
            jax.ShapeDtypeStruct((2 * chips, slots * rows, lanes), amplitudes.dtype),
            jax.ShapeDtypeStruct((tiles + 1,), jnp.int32),
        ),
        scratch_shapes=[pltpu.VMEM((irreps, rows, lanes), jnp.float32)],
    )(labels, amplitudes)


def half_kernel(where_ref, integrals_ref, block_ref, previous_ref, side, begin, strip_ref, out_ref, sems):
    tiles, _, half = strip_ref.shape
    chunk = 256
    copies = []
    for t in range(tiles):
        slot = where_ref[t]
        for offset in range(0, half, chunk):
            columns = pl.ds(pl.multiple_of(begin + offset, chunk), chunk)
            product = jnp.dot(
                integrals_ref[t], block_ref[slot, :, offset : offset + chunk], preferred_element_type=jnp.float32
            )
            total = previous_ref[t, :, columns].astype(jnp.float32) + product
            strip_ref[t, :, offset : offset + chunk] = total.astype(strip_ref.dtype)
        target = out_ref.at[t, :, pl.ds(pl.multiple_of(side * half, half), half)]
        copies.append(pltpu.make_async_copy(strip_ref.at[t], target, sems.at[t]))
        copies[-1].start()
    return copies


def own_kernel(
    where_ref, integrals_ref, block_ref, previous_ref, out_ref, kept_integrals_ref, kept_previous_ref, strip_ref, sems
):
    half = block_ref.shape[2]
    side = lax.axis_index("core")
    copies = half_kernel(where_ref, integrals_ref, block_ref, previous_ref, side, side * half, strip_ref, out_ref, sems)
    kept_integrals_ref[...] = integrals_ref[...]
    kept_previous_ref[...] = previous_ref[:, :, pl.ds(pl.multiple_of((1 - side) * half, half), half)]
    for copy in copies:
        copy.wait()


def other_kernel(where_ref, integrals_ref, block_ref, previous_ref, so_far_ref, out_ref, strip_ref, sems):
    side = 1 - lax.axis_index("core")
    for copy in half_kernel(where_ref, integrals_ref, block_ref, previous_ref, side, 0, strip_ref, out_ref, sems):
        copy.wait()


def scratch(tiles, rows, half, dtype):
    return [pltpu.VMEM((tiles, rows, half), dtype), pltpu.SemaphoreType.DMA((tiles,))]


def own_half(where, integrals, block, residual_in):
    tiles, rows, depth = integrals.shape
    half = block.shape[2]
    return pl.pallas_call(
        own_kernel,
        in_specs=[SMEM, VMEM, VMEM, VMEM],
        out_specs=(ANY, VMEM, VMEM),
        out_shape=(
            jax.ShapeDtypeStruct(residual_in.shape, residual_in.dtype),
            jax.ShapeDtypeStruct(integrals.shape, integrals.dtype),
            jax.ShapeDtypeStruct((tiles, rows, half), residual_in.dtype),
        ),
        scratch_shapes=scratch(tiles, rows, half, residual_in.dtype),
        cost_estimate=pl.CostEstimate(
            flops=2 * tiles * rows * depth * half, bytes_accessed=4_000_000, transcendentals=0
        ),
        compiler_params=pltpu.CompilerParams(vmem_limit_bytes=24 * 2**20),
    )(where, integrals, block, residual_in)


def other_half(where, integrals, block, previous, so_far):
    return pl.pallas_call(
        other_kernel,
        in_specs=[SMEM, VMEM, VMEM, VMEM, ANY],
        out_specs=ANY,
        out_shape=jax.ShapeDtypeStruct(so_far.shape, so_far.dtype),
        scratch_shapes=scratch(*previous.shape, so_far.dtype),
        input_output_aliases={4: 0},
        compiler_params=pltpu.CompilerParams(vmem_limit_bytes=24 * 2**20),
    )(where, integrals, block, previous, so_far)


def put(whole, block, at):
    return lax.dynamic_update_slice_in_dim(whole, block[:, None], lax.rem(at + whole.shape[1], whole.shape[1]), 1)


def with_slots(slots, incoming, where, integrals, residual_in, depth, width):
    half = lax.axis_size("chip")
    core = lax.axis_index("core")
    parts = incoming.shape[2] // width
    every = incoming.reshape(2, half, slots, depth // parts, parts, width).transpose(0, 2, 4, 3, 1, 5)
    every = every.reshape(2, slots, depth, half * width)
    mine = lax.dynamic_index_in_dim(every, core, 0, keepdims=False)
    z_size, z = lax.axis_size("bulk_1"), lax.axis_index("bulk_1")
    ways = [(c, i, (i + 1 - 2 * c) % z_size) for c in range(2) for i in range(z_size)]
    same = [(c * z_size + i, c * z_size + to) for c, i, to in ways]
    across = [(c * z_size + i, (1 - c) * z_size + to) for c, i, to in ways]
    near = lax.ppermute(mine, ("core", "bulk_1"), same)
    theirs = lax.dynamic_index_in_dim(every, 1 - core, 0, keepdims=False)
    opposite = lax.ppermute(theirs, ("core", "bulk_1"), across)
    group = jnp.zeros((slots, z_size, depth, half * width), mine.dtype)
    way = 1 - 2 * core
    group = put(put(put(group, mine, z), near, z - way), opposite, z + way)
    group = group.reshape(slots, z_size * depth, half * width)
    y_size, y = lax.axis_size("bulk_0"), lax.axis_index("bulk_0")
    whole = jnp.zeros((slots, y_size, z_size * depth, half * width), mine.dtype)
    whole = put(whole, group, y)
    up, down = group, group
    for step in range(1, y_size // 2 - 1):
        up, down = shift(up, "bulk_0", 1), shift(down, "bulk_0", -1)
        whole = put(put(whole, up, y - step), down, y + step)
    last = y_size // 2 - 1
    far, up, down = shift(down, "bulk_0", -2), shift(up, "bulk_0", 1), shift(down, "bulk_0", -1)
    whole = put(put(put(whole, up, y - last), down, y + last), far, y + last + 1)
    other = shift(whole, "core", 1)
    flat = (slots, y_size * z_size * depth, half * width)
    out, integrals, previous = own_half(where, integrals, whole.reshape(flat), residual_in)
    return other_half(where, integrals, other.reshape(flat), previous, out)


def local(integrals, amplitudes, residual_in, tile_irrep):
    tiles = integrals.shape[0]
    _, depth, width = amplitudes.shape

    def spread(outgoing):
        return lax.all_to_all(outgoing, CHIP_CORE, split_axis=0, concat_axis=0, tiled=True)

    outgoing, where = choose(2, tile_irrep, amplitudes, tiles)
    incoming = spread(outgoing)

    def two():
        return with_slots(2, incoming, where, integrals, residual_in, depth, width)

    def three():
        wider = spread(choose(3, tile_irrep, amplitudes, tiles)[0])
        return with_slots(3, wider, where, integrals, residual_in, depth, width)

    return lax.cond(where[tiles] > 2, three, two)


def solution(mesh):
    tile, bulk = mesh.shape["tile"], mesh.shape["bulk"]
    finer = Mesh(mesh.devices.reshape(tile // 2, 2, bulk // 3, 3), TILE_BULK)
    placed = (P(TILE_BULK, None, None), P(None, BULK, CHIP_CORE), P(TILE_BULK, None, None), P())
    return jax.shard_map(
        local, mesh=finer, in_specs=placed, out_specs=P(TILE_BULK, None, None), check_vma=False
    )
```

```python
import functools

import jax
import jax.numpy as jnp
from jax import lax
from jax.experimental import pallas as pl
from jax.experimental.pallas import tpu as pltpu
from jax.sharding import Mesh
from jax.sharding import PartitionSpec as P

CHIP_CORE = ("chip", "core")
TILE_BULK = ("chip", "core", "bulk_0", "bulk_1")
BULK = ("bulk_0", "bulk_1")
VMEM = pl.BlockSpec(memory_space=pltpu.VMEM)
SMEM = pl.BlockSpec(memory_space=pltpu.SMEM)
ANY = pl.BlockSpec(memory_space=pl.ANY)


def shift(value, axis, step):
    size = lax.axis_size(axis)
    return lax.ppermute(value, axis, [(i, (i + step) % size) for i in range(size)])


def choose_kernel(slots, chips, tiles, bulk_0, bulk_1, labels_ref, amplitudes_ref, outgoing_ref, where_ref, packed_ref):
    per_chip = labels_ref.shape[0] // chips
    irreps, rows, lanes = packed_ref.shape
    for irrep in range(irreps):
        block = amplitudes_ref[irrep].astype(jnp.float32)
        pieces = [block[begin : begin + rows] for begin in range(0, block.shape[0], rows)]
        packed_ref[irrep] = jnp.concatenate(pieces, axis=1)
    most = jnp.int32(0)
    for chip in range(chips):
        first, last = labels_ref[chip * per_chip], labels_ref[(chip + 1) * per_chip - 1]
        most = jnp.maximum(most, last - first)
        chosen = [packed_ref[jnp.minimum(first + slot, last)] for slot in range(slots)]
        chosen = jnp.concatenate(chosen, axis=0).astype(outgoing_ref.dtype)
        for core in range(2):
            outgoing_ref[2 * chip + core] = chosen
    own = lax.axis_index("chip")
    row = own * 2 + lax.axis_index("core")
    column = lax.axis_index("bulk_0") * bulk_1 + lax.axis_index("bulk_1")
    first_tile = (row * (bulk_0 * bulk_1) + column) * tiles
    for t in range(tiles):
        where_ref[t] = labels_ref[first_tile + t] - labels_ref[own * per_chip]
    where_ref[tiles] = most + 1


def choose(slots, labels, amplitudes, tiles):
    chips = lax.axis_size("chip")
    irreps, depth, width = amplitudes.shape
    lanes = 128
    rows = depth * width // lanes
    body = functools.partial(
        choose_kernel, slots, chips, tiles, lax.axis_size("bulk_0"), lax.axis_size("bulk_1")
    )
    return pl.pallas_call(
        body,
        in_specs=[SMEM, VMEM],
        out_specs=(VMEM, SMEM),
        out_shape=(
            jax.ShapeDtypeStruct((2 * chips, slots * rows, lanes), amplitudes.dtype),
            jax.ShapeDtypeStruct((tiles + 1,), jnp.int32),
        ),
        scratch_shapes=[pltpu.VMEM((irreps, rows, lanes), jnp.float32)],
    )(labels, amplitudes)


def half_kernel(where_ref, integrals_ref, block_ref, previous_ref, side, begin, strip_ref, out_ref, sems):
    tiles, _, half = strip_ref.shape
    chunk = 256
    copies = []
    for t in range(tiles):
        slot = where_ref[t]
        for offset in range(0, half, chunk):
            columns = pl.ds(pl.multiple_of(begin + offset, chunk), chunk)
            product = jnp.dot(
                integrals_ref[t], block_ref[slot, :, offset : offset + chunk], preferred_element_type=jnp.float32
            )
            total = previous_ref[t, :, columns].astype(jnp.float32) + product
            strip_ref[t, :, offset : offset + chunk] = total.astype(strip_ref.dtype)
        target = out_ref.at[t, :, pl.ds(pl.multiple_of(side * half, half), half)]
        copies.append(pltpu.make_async_copy(strip_ref.at[t], target, sems.at[t]))
        copies[-1].start()
    return copies


def own_kernel(
    where_ref, integrals_ref, block_ref, previous_ref, out_ref, kept_integrals_ref, kept_previous_ref, strip_ref, sems
):
    half = block_ref.shape[2]
    side = lax.axis_index("core")
    copies = half_kernel(where_ref, integrals_ref, block_ref, previous_ref, side, side * half, strip_ref, out_ref, sems)
    kept_integrals_ref[...] = integrals_ref[...]
    kept_previous_ref[...] = previous_ref[:, :, pl.ds(pl.multiple_of((1 - side) * half, half), half)]
    for copy in copies:
        copy.wait()


def other_kernel(where_ref, integrals_ref, block_ref, previous_ref, so_far_ref, out_ref, strip_ref, sems):
    side = 1 - lax.axis_index("core")
    for copy in half_kernel(where_ref, integrals_ref, block_ref, previous_ref, side, 0, strip_ref, out_ref, sems):
        copy.wait()


def scratch(tiles, rows, half, dtype):
    return [pltpu.VMEM((tiles, rows, half), dtype), pltpu.SemaphoreType.DMA((tiles,))]


def own_half(where, integrals, block, residual_in):
    tiles, rows, depth = integrals.shape
    half = block.shape[2]
    return pl.pallas_call(
        own_kernel,
        in_specs=[SMEM, VMEM, VMEM, VMEM],
        out_specs=(ANY, VMEM, VMEM),
        out_shape=(
            jax.ShapeDtypeStruct(residual_in.shape, residual_in.dtype),
            jax.ShapeDtypeStruct(integrals.shape, integrals.dtype),
            jax.ShapeDtypeStruct((tiles, rows, half), residual_in.dtype),
        ),
        scratch_shapes=scratch(tiles, rows, half, residual_in.dtype),
        cost_estimate=pl.CostEstimate(
            flops=2 * tiles * rows * depth * half, bytes_accessed=4_000_000, transcendentals=0
        ),
        compiler_params=pltpu.CompilerParams(vmem_limit_bytes=24 * 2**20),
    )(where, integrals, block, residual_in)


def other_half(where, integrals, block, previous, so_far):
    return pl.pallas_call(
        other_kernel,
        in_specs=[SMEM, VMEM, VMEM, VMEM, ANY],
        out_specs=ANY,
        out_shape=jax.ShapeDtypeStruct(so_far.shape, so_far.dtype),
        scratch_shapes=scratch(*previous.shape, so_far.dtype),
        input_output_aliases={4: 0},
        compiler_params=pltpu.CompilerParams(vmem_limit_bytes=24 * 2**20),
    )(where, integrals, block, previous, so_far)


def turn(value, step):
    size = lax.axis_size("bulk_0")
    pairs = [(c * size + i, c * size + (i + (1 - 2 * c) * step) % size) for c in range(2) for i in range(size)]
    return lax.ppermute(value, ("core", "bulk_0"), pairs)


def put(whole, block, at):
    return lax.dynamic_update_slice_in_dim(whole, block[:, None], lax.rem(at + whole.shape[1], whole.shape[1]), 1)


def with_slots(slots, incoming, where, integrals, residual_in, depth, width):
    half = lax.axis_size("chip")
    core = lax.axis_index("core")
    parts = incoming.shape[2] // width
    every = incoming.reshape(2, half, slots, depth // parts, parts, width).transpose(0, 2, 4, 3, 1, 5)
    every = every.reshape(2, slots, depth, half * width)
    mine = lax.dynamic_index_in_dim(every, core, 0, keepdims=False)
    z_size, z = lax.axis_size("bulk_1"), lax.axis_index("bulk_1")
    ways = [(c, i, (i + 1 - 2 * c) % z_size) for c in range(2) for i in range(z_size)]
    same = [(c * z_size + i, c * z_size + to) for c, i, to in ways]
    across = [(c * z_size + i, (1 - c) * z_size + to) for c, i, to in ways]
    near = lax.ppermute(mine, ("core", "bulk_1"), same)
    theirs = lax.dynamic_index_in_dim(every, 1 - core, 0, keepdims=False)
    opposite = lax.ppermute(theirs, ("core", "bulk_1"), across)
    group = jnp.zeros((slots, z_size, depth, half * width), mine.dtype)
    way = 1 - 2 * core
    group = put(put(put(group, mine, z), near, z - way), opposite, z + way)
    group = group.reshape(slots, z_size * depth, half * width)
    y_size, y = lax.axis_size("bulk_0"), lax.axis_index("bulk_0")
    whole = jnp.zeros((slots, y_size, z_size * depth, half * width), mine.dtype)
    whole = put(whole, group, y)
    first, second = group, group
    for step in range(1, y_size // 2 - 1):
        first, second = turn(first, -1), turn(second, 1)
        whole = put(put(whole, second, y - way * step), first, y + way * step)
    last = y_size // 2 - 1
    far, second, first = turn(first, -2), turn(second, 1), turn(first, -1)
    whole = put(put(put(whole, second, y - way * last), first, y + way * last), far, y + last + 1)
    other = shift(whole, "core", 1)
    flat = (slots, y_size * z_size * depth, half * width)
    out, integrals, previous = own_half(where, integrals, whole.reshape(flat), residual_in)
    return other_half(where, integrals, other.reshape(flat), previous, out)


def local(integrals, amplitudes, residual_in, tile_irrep):
    tiles = integrals.shape[0]
    _, depth, width = amplitudes.shape

    def spread(outgoing):
        return lax.all_to_all(outgoing, CHIP_CORE, split_axis=0, concat_axis=0, tiled=True)

    outgoing, where = choose(2, tile_irrep, amplitudes, tiles)
    incoming = spread(outgoing)

    def two():
        return with_slots(2, incoming, where, integrals, residual_in, depth, width)

    def three():
        wider = spread(choose(3, tile_irrep, amplitudes, tiles)[0])
        return with_slots(3, wider, where, integrals, residual_in, depth, width)

    return lax.cond(where[tiles] > 2, three, two)


def solution(mesh):
    tile, bulk = mesh.shape["tile"], mesh.shape["bulk"]
    finer = Mesh(mesh.devices.reshape(tile // 2, 2, bulk // 3, 3), TILE_BULK)
    placed = (P(TILE_BULK, None, None), P(None, BULK, CHIP_CORE), P(TILE_BULK, None, None), P())
    return jax.shard_map(
        local, mesh=finer, in_specs=placed, out_specs=P(TILE_BULK, None, None), check_vma=False
    )
```

```python
import functools

import jax
import jax.numpy as jnp
from jax import lax
from jax.experimental import pallas as pl
from jax.experimental.pallas import tpu as pltpu
from jax.sharding import Mesh
from jax.sharding import PartitionSpec as P

CHIP_CORE = ("chip", "core")
TILE_BULK = ("chip", "core", "bulk_0", "bulk_1")
BULK = ("bulk_0", "bulk_1")
VMEM = pl.BlockSpec(memory_space=pltpu.VMEM)
SMEM = pl.BlockSpec(memory_space=pltpu.SMEM)
ANY = pl.BlockSpec(memory_space=pl.ANY)


def shift(value, axis, step):
    size = lax.axis_size(axis)
    return lax.ppermute(value, axis, [(i, (i + step) % size) for i in range(size)])


def choose_kernel(slots, chips, tiles, bulk_0, bulk_1, labels_ref, amplitudes_ref, outgoing_ref, where_ref, packed_ref):
    per_chip = labels_ref.shape[0] // chips
    irreps, rows, lanes = packed_ref.shape
    for irrep in range(irreps):
        block = amplitudes_ref[irrep].astype(jnp.float32)
        pieces = [block[begin : begin + rows] for begin in range(0, block.shape[0], rows)]
        packed_ref[irrep] = jnp.concatenate(pieces, axis=1)
    most = jnp.int32(0)
    for chip in range(chips):
        first, last = labels_ref[chip * per_chip], labels_ref[(chip + 1) * per_chip - 1]
        most = jnp.maximum(most, last - first)
        chosen = [packed_ref[jnp.minimum(first + slot, last)] for slot in range(slots)]
        chosen = jnp.concatenate(chosen, axis=0).astype(outgoing_ref.dtype)
        for core in range(2):
            outgoing_ref[2 * chip + core] = chosen
    own = lax.axis_index("chip")
    row = own * 2 + lax.axis_index("core")
    column = lax.axis_index("bulk_0") * bulk_1 + lax.axis_index("bulk_1")
    first_tile = (row * (bulk_0 * bulk_1) + column) * tiles
    for t in range(tiles):
        where_ref[t] = labels_ref[first_tile + t] - labels_ref[own * per_chip]
    where_ref[tiles] = most + 1


def choose(slots, labels, amplitudes, tiles):
    chips = lax.axis_size("chip")
    irreps, depth, width = amplitudes.shape
    lanes = 128
    rows = depth * width // lanes
    body = functools.partial(
        choose_kernel, slots, chips, tiles, lax.axis_size("bulk_0"), lax.axis_size("bulk_1")
    )
    return pl.pallas_call(
        body,
        in_specs=[SMEM, VMEM],
        out_specs=(VMEM, SMEM),
        out_shape=(
            jax.ShapeDtypeStruct((2 * chips, slots * rows, lanes), amplitudes.dtype),
            jax.ShapeDtypeStruct((tiles + 1,), jnp.int32),
        ),
        scratch_shapes=[pltpu.VMEM((irreps, rows, lanes), jnp.float32)],
    )(labels, amplitudes)


def half_kernel(where_ref, integrals_ref, block_ref, previous_ref, side, begin, strip_ref, out_ref, sems):
    tiles, _, half = strip_ref.shape
    chunk = 256
    copies = []
    for t in range(tiles):
        slot = where_ref[t]
        for offset in range(0, half, chunk):
            columns = pl.ds(pl.multiple_of(begin + offset, chunk), chunk)
            product = jnp.dot(
                integrals_ref[t], block_ref[slot, :, offset : offset + chunk], preferred_element_type=jnp.float32
            )
            total = previous_ref[t, :, columns].astype(jnp.float32) + product
            strip_ref[t, :, offset : offset + chunk] = total.astype(strip_ref.dtype)
        target = out_ref.at[t, :, pl.ds(pl.multiple_of(side * half, half), half)]
        copies.append(pltpu.make_async_copy(strip_ref.at[t], target, sems.at[t]))
        copies[-1].start()
    return copies


def own_kernel(
    where_ref, integrals_ref, block_ref, previous_ref, out_ref, kept_integrals_ref, kept_previous_ref, strip_ref, sems
):
    half = block_ref.shape[2]
    side = lax.axis_index("core")
    copies = half_kernel(where_ref, integrals_ref, block_ref, previous_ref, side, side * half, strip_ref, out_ref, sems)
    kept_integrals_ref[...] = integrals_ref[...]
    kept_previous_ref[...] = previous_ref[:, :, pl.ds(pl.multiple_of((1 - side) * half, half), half)]
    for copy in copies:
        copy.wait()


def other_kernel(where_ref, integrals_ref, block_ref, previous_ref, so_far_ref, out_ref, strip_ref, sems):
    side = 1 - lax.axis_index("core")
    for copy in half_kernel(where_ref, integrals_ref, block_ref, previous_ref, side, 0, strip_ref, out_ref, sems):
        copy.wait()


def scratch(tiles, rows, half, dtype):
    return [pltpu.VMEM((tiles, rows, half), dtype), pltpu.SemaphoreType.DMA((tiles,))]


def own_half(where, integrals, block, residual_in):
    tiles, rows, depth = integrals.shape
    half = block.shape[2]
    return pl.pallas_call(
        own_kernel,
        in_specs=[SMEM, VMEM, VMEM, VMEM],
        out_specs=(ANY, VMEM, VMEM),
        out_shape=(
            jax.ShapeDtypeStruct(residual_in.shape, residual_in.dtype),
            jax.ShapeDtypeStruct(integrals.shape, integrals.dtype),
            jax.ShapeDtypeStruct((tiles, rows, half), residual_in.dtype),
        ),
        scratch_shapes=scratch(tiles, rows, half, residual_in.dtype),
        cost_estimate=pl.CostEstimate(
            flops=2 * tiles * rows * depth * half, bytes_accessed=4_000_000, transcendentals=0
        ),
        compiler_params=pltpu.CompilerParams(vmem_limit_bytes=24 * 2**20),
    )(where, integrals, block, residual_in)


def other_half(where, integrals, block, previous, so_far):
    return pl.pallas_call(
        other_kernel,
        in_specs=[SMEM, VMEM, VMEM, VMEM, ANY],
        out_specs=ANY,
        out_shape=jax.ShapeDtypeStruct(so_far.shape, so_far.dtype),
        scratch_shapes=scratch(*previous.shape, so_far.dtype),
        input_output_aliases={4: 0},
        compiler_params=pltpu.CompilerParams(vmem_limit_bytes=24 * 2**20),
    )(where, integrals, block, previous, so_far)


def turn(value, step):
    size = lax.axis_size("bulk_0")
    pairs = [(c * size + i, c * size + (i + (1 - 2 * c) * step) % size) for c in range(2) for i in range(size)]
    return lax.ppermute(value, ("core", "bulk_0"), pairs)


def put(whole, block, at):
    return lax.dynamic_update_slice_in_dim(whole, block[:, None], lax.rem(at + whole.shape[1], whole.shape[1]), 1)


def with_slots(slots, incoming, where, integrals, residual_in, depth, width):
    half = lax.axis_size("chip")
    core = lax.axis_index("core")
    parts = incoming.shape[2] // width
    every = incoming.reshape(2, half, slots, depth // parts, parts, width).transpose(0, 2, 4, 3, 1, 5)
    every = every.reshape(2, slots, depth, half * width)
    mine = lax.dynamic_index_in_dim(every, core, 0, keepdims=False)
    z_size, z = lax.axis_size("bulk_1"), lax.axis_index("bulk_1")
    ways = [(c, i, (i + 1 - 2 * c) % z_size) for c in range(2) for i in range(z_size)]
    same = [(c * z_size + i, c * z_size + to) for c, i, to in ways]
    across = [(c * z_size + i, (1 - c) * z_size + to) for c, i, to in ways]
    near = lax.ppermute(mine, ("core", "bulk_1"), same)
    theirs = lax.dynamic_index_in_dim(every, 1 - core, 0, keepdims=False)
    opposite = lax.ppermute(theirs, ("core", "bulk_1"), across)
    group = jnp.zeros((slots, z_size, depth, half * width), mine.dtype)
    way = 1 - 2 * core
    group = put(put(put(group, mine, z), near, z - way), opposite, z + way)
    group = group.reshape(slots, z_size * depth, half * width)
    y_size, y = lax.axis_size("bulk_0"), lax.axis_index("bulk_0")
    whole = jnp.zeros((slots, y_size, z_size * depth, half * width), mine.dtype)
    whole = put(whole, group, y)
    first, second = group, group
    for step in range(1, y_size // 2 - 1):
        first, second = turn(first, -1), turn(second, 1)
        whole = put(put(whole, second, y - way * step), first, y + way * step)
        if step == 1:
            far = turn(first, step - y_size // 2)
    last = y_size // 2 - 1
    second, first = turn(second, 1), turn(first, -1)
    whole = put(put(put(whole, second, y - way * last), first, y + way * last), far, y + last + 1)
    other = shift(whole, "core", 1)
    flat = (slots, y_size * z_size * depth, half * width)
    out, integrals, previous = own_half(where, integrals, whole.reshape(flat), residual_in)
    return other_half(where, integrals, other.reshape(flat), previous, out)


def local(integrals, amplitudes, residual_in, tile_irrep):
    tiles = integrals.shape[0]
    _, depth, width = amplitudes.shape

    def spread(outgoing):
        return lax.all_to_all(outgoing, CHIP_CORE, split_axis=0, concat_axis=0, tiled=True)

    outgoing, where = choose(2, tile_irrep, amplitudes, tiles)
    incoming = spread(outgoing)

    def two():
        return with_slots(2, incoming, where, integrals, residual_in, depth, width)

    def three():
        wider = spread(choose(3, tile_irrep, amplitudes, tiles)[0])
        return with_slots(3, wider, where, integrals, residual_in, depth, width)

    return lax.cond(where[tiles] > 2, three, two)


def solution(mesh):
    tile, bulk = mesh.shape["tile"], mesh.shape["bulk"]
    finer = Mesh(mesh.devices.reshape(tile // 2, 2, bulk // 3, 3), TILE_BULK)
    placed = (P(TILE_BULK, None, None), P(None, BULK, CHIP_CORE), P(TILE_BULK, None, None), P())
    return jax.shard_map(
        local, mesh=finer, in_specs=placed, out_specs=P(TILE_BULK, None, None), check_vma=False
    )
```

```python
import functools

import jax
import jax.numpy as jnp
from jax import lax
from jax.experimental import pallas as pl
from jax.experimental.pallas import tpu as pltpu
from jax.sharding import Mesh
from jax.sharding import PartitionSpec as P

CHIP_CORE = ("chip", "core")
TILE_BULK = ("chip", "core", "bulk_0", "bulk_1")
BULK = ("bulk_0", "bulk_1")
VMEM = pl.BlockSpec(memory_space=pltpu.VMEM)
SMEM = pl.BlockSpec(memory_space=pltpu.SMEM)
ANY = pl.BlockSpec(memory_space=pl.ANY)


def shift(value, axis, step):
    size = lax.axis_size(axis)
    return lax.ppermute(value, axis, [(i, (i + step) % size) for i in range(size)])


def choose_kernel(slots, chips, tiles, bulk_0, bulk_1, labels_ref, amplitudes_ref, outgoing_ref, where_ref, packed_ref):
    per_chip = labels_ref.shape[0] // chips
    irreps, rows, lanes = packed_ref.shape
    for irrep in range(irreps):
        block = amplitudes_ref[irrep].astype(jnp.float32)
        pieces = [block[begin : begin + rows] for begin in range(0, block.shape[0], rows)]
        packed_ref[irrep] = jnp.concatenate(pieces, axis=1)
    most = jnp.int32(0)
    for chip in range(chips):
        first, last = labels_ref[chip * per_chip], labels_ref[(chip + 1) * per_chip - 1]
        most = jnp.maximum(most, last - first)
        chosen = [packed_ref[jnp.minimum(first + slot, last)] for slot in range(slots)]
        chosen = jnp.concatenate(chosen, axis=0).astype(outgoing_ref.dtype)
        for core in range(2):
            outgoing_ref[2 * chip + core] = chosen
    own = lax.axis_index("chip")
    row = own * 2 + lax.axis_index("core")
    column = lax.axis_index("bulk_0") * bulk_1 + lax.axis_index("bulk_1")
    first_tile = (row * (bulk_0 * bulk_1) + column) * tiles
    for t in range(tiles):
        where_ref[t] = labels_ref[first_tile + t] - labels_ref[own * per_chip]
    where_ref[tiles] = most + 1


def choose(slots, labels, amplitudes, tiles):
    chips = lax.axis_size("chip")
    irreps, depth, width = amplitudes.shape
    lanes = 128
    rows = depth * width // lanes
    body = functools.partial(
        choose_kernel, slots, chips, tiles, lax.axis_size("bulk_0"), lax.axis_size("bulk_1")
    )
    return pl.pallas_call(
        body,
        in_specs=[SMEM, VMEM],
        out_specs=(VMEM, SMEM),
        out_shape=(
            jax.ShapeDtypeStruct((2 * chips, slots * rows, lanes), amplitudes.dtype),
            jax.ShapeDtypeStruct((tiles + 1,), jnp.int32),
        ),
        scratch_shapes=[pltpu.VMEM((irreps, rows, lanes), jnp.float32)],
    )(labels, amplitudes)


def half_kernel(where_ref, integrals_ref, block_ref, previous_ref, side, begin, strip_ref, out_ref, sems):
    tiles, _, half = strip_ref.shape
    chunk = 256
    copies = []
    for t in range(tiles):
        slot = where_ref[t]
        for offset in range(0, half, chunk):
            columns = pl.ds(pl.multiple_of(begin + offset, chunk), chunk)
            product = jnp.dot(
                integrals_ref[t], block_ref[slot, :, offset : offset + chunk], preferred_element_type=jnp.float32
            )
            total = previous_ref[t, :, columns].astype(jnp.float32) + product
            strip_ref[t, :, offset : offset + chunk] = total.astype(strip_ref.dtype)
        target = out_ref.at[t, :, pl.ds(pl.multiple_of(side * half, half), half)]
        copies.append(pltpu.make_async_copy(strip_ref.at[t], target, sems.at[t]))
        copies[-1].start()
    return copies


def own_kernel(
    where_ref, integrals_ref, block_ref, previous_ref, out_ref, kept_integrals_ref, kept_previous_ref, strip_ref, sems
):
    half = block_ref.shape[2]
    side = lax.axis_index("core")
    copies = half_kernel(where_ref, integrals_ref, block_ref, previous_ref, side, side * half, strip_ref, out_ref, sems)
    kept_integrals_ref[...] = integrals_ref[...]
    kept_previous_ref[...] = previous_ref[:, :, pl.ds(pl.multiple_of((1 - side) * half, half), half)]
    for copy in copies:
        copy.wait()


def other_kernel(where_ref, integrals_ref, block_ref, previous_ref, so_far_ref, out_ref, strip_ref, sems):
    side = 1 - lax.axis_index("core")
    for copy in half_kernel(where_ref, integrals_ref, block_ref, previous_ref, side, 0, strip_ref, out_ref, sems):
        copy.wait()


def scratch(tiles, rows, half, dtype):
    return [pltpu.VMEM((tiles, rows, half), dtype), pltpu.SemaphoreType.DMA((tiles,))]


def own_half(where, integrals, block, residual_in):
    tiles, rows, depth = integrals.shape
    half = block.shape[2]
    return pl.pallas_call(
        own_kernel,
        in_specs=[SMEM, VMEM, VMEM, VMEM],
        out_specs=(ANY, VMEM, VMEM),
        out_shape=(
            jax.ShapeDtypeStruct(residual_in.shape, residual_in.dtype),
            jax.ShapeDtypeStruct(integrals.shape, integrals.dtype),
            jax.ShapeDtypeStruct((tiles, rows, half), residual_in.dtype),
        ),
        scratch_shapes=scratch(tiles, rows, half, residual_in.dtype),
        cost_estimate=pl.CostEstimate(
            flops=2 * tiles * rows * depth * half, bytes_accessed=4_000_000, transcendentals=0
        ),
        compiler_params=pltpu.CompilerParams(vmem_limit_bytes=24 * 2**20),
    )(where, integrals, block, residual_in)


def other_half(where, integrals, block, previous, so_far):
    return pl.pallas_call(
        other_kernel,
        in_specs=[SMEM, VMEM, VMEM, VMEM, ANY],
        out_specs=ANY,
        out_shape=jax.ShapeDtypeStruct(so_far.shape, so_far.dtype),
        scratch_shapes=scratch(*previous.shape, so_far.dtype),
        input_output_aliases={4: 0},
        compiler_params=pltpu.CompilerParams(vmem_limit_bytes=24 * 2**20),
    )(where, integrals, block, previous, so_far)


def turn(value, step):
    size = lax.axis_size("bulk_0")
    pairs = [(c * size + i, c * size + (i + (1 - 2 * c) * step) % size) for c in range(2) for i in range(size)]
    return lax.ppermute(value, ("core", "bulk_0"), pairs)


def put(whole, block, at):
    return lax.dynamic_update_slice_in_dim(whole, block[:, None], lax.rem(at + whole.shape[1], whole.shape[1]), 1)


def with_slots(slots, incoming, where, integrals, residual_in, depth, width):
    half = lax.axis_size("chip")
    core = lax.axis_index("core")
    mine = lax.dynamic_slice_in_dim(incoming, core * half, half, 0)
    parts = incoming.shape[2] // width
    mine = mine.reshape(half, slots, depth // parts, parts, width).transpose(1, 3, 2, 0, 4)
    mine = mine.reshape(slots, depth, half * width)
    z_size, z = lax.axis_size("bulk_1"), lax.axis_index("bulk_1")
    group = jnp.zeros((slots, z_size, depth, half * width), mine.dtype)
    group = lax.dynamic_update_slice_in_dim(group, mine[:, None], z, 1)
    for step in range(1, z_size):
        got = shift(mine, "bulk_1", step)
        group = lax.dynamic_update_slice_in_dim(group, got[:, None], lax.rem(z - step + z_size, z_size), 1)
    group = group.reshape(slots, z_size * depth, half * width)
    way = 1 - 2 * core
    y_size, y = lax.axis_size("bulk_0"), lax.axis_index("bulk_0")
    whole = jnp.zeros((slots, y_size, z_size * depth, half * width), mine.dtype)
    whole = put(whole, group, y)
    first, second = group, group
    for step in range(1, y_size // 2 - 1):
        first, second = turn(first, -1), turn(second, 1)
        whole = put(put(whole, second, y - way * step), first, y + way * step)
    last = y_size // 2 - 1
    far, second, first = turn(first, -2), turn(second, 1), turn(first, -1)
    whole = put(put(put(whole, second, y - way * last), first, y + way * last), far, y + last + 1)
    other = shift(whole, "core", 1)
    flat = (slots, y_size * z_size * depth, half * width)
    out, integrals, previous = own_half(where, integrals, whole.reshape(flat), residual_in)
    return other_half(where, integrals, other.reshape(flat), previous, out)


def local(integrals, amplitudes, residual_in, tile_irrep):
    tiles = integrals.shape[0]
    _, depth, width = amplitudes.shape

    def spread(outgoing):
        return lax.all_to_all(outgoing, CHIP_CORE, split_axis=0, concat_axis=0, tiled=True)

    outgoing, where = choose(2, tile_irrep, amplitudes, tiles)
    incoming = spread(outgoing)

    def two():
        return with_slots(2, incoming, where, integrals, residual_in, depth, width)

    def three():
        wider = spread(choose(3, tile_irrep, amplitudes, tiles)[0])
        return with_slots(3, wider, where, integrals, residual_in, depth, width)

    return lax.cond(where[tiles] > 2, three, two)


def solution(mesh):
    tile, bulk = mesh.shape["tile"], mesh.shape["bulk"]
    finer = Mesh(mesh.devices.reshape(tile // 2, 2, bulk // 3, 3), TILE_BULK)
    placed = (P(TILE_BULK, None, None), P(None, BULK, CHIP_CORE), P(TILE_BULK, None, None), P())
    return jax.shard_map(
        local, mesh=finer, in_specs=placed, out_specs=P(TILE_BULK, None, None), check_vma=False
    )
```
